32 devices in a mesh: dp: 8 (over z, y), tensor: 4 (over x, core).
Axes of the slice: x: 2, y: 2, z: 4, core: 2. Of those that a mesh axis runs over, the one named last changes fastest.
Arguments:
- residual: bfloat16 [1024, 2048], P(('dp', 'tensor')), may hold values from -6 to 6
- norm_gain: float32 [2048], replicated, may hold values from 0.1 to 1.9
- gate_weight: bfloat16 [2048, 7168], P(None, 'tensor'), may hold values from -0.125 to 0.125
- up_weight: bfloat16 [2048, 7168], P(None, 'tensor'), may hold values from -0.125 to 0.125
- hidden_grad: bfloat16 [1024, 7168], P('dp', 'tensor'), may hold values from -6 to 6
Outputs:
- residual_grad: bfloat16 [1024, 2048], P(('dp', 'tensor'))
- gate_weight_grad: bfloat16 [2048, 7168], P('dp', 'tensor')
- up_weight_grad: bfloat16 [2048, 7168], P('dp', 'tensor')
The draws below stay inside these ranges and needn't reach their ends.
All inputs are finite; a program needn't handle non-finite values.
Results may differ from the reference program's by a relative error of at most 0.024.
Values may be sent and summed in bfloat16 or wider, within the bound.
A program may use at most 64 MiB of HBM per device.

```python
import math
import jax
import jax.numpy as jnp
from jax import lax

D = 2048
FF = 7168
ROWS = 128
TOKENS = 1024
N_DP = 8
N_TENSOR = 4


def block_levels(rng, extent, split, smallest, high):
    level, own = 1.0, jax.random.fold_in(rng, 6)
    for axis_at, shards_of in split:
        heights = jnp.exp(jax.random.uniform(jax.random.fold_in(own, axis_at), (shards_of,), jnp.float32, smallest / len(split), high / len(split)))
        level = level * jnp.repeat(heights, extent[axis_at] // shards_of).reshape([-1 if axis == axis_at else 1 for axis in range(len(extent))])
    return level


def gaussian(own_key, dims, scale, most, split=(), held_as=jnp.bfloat16):
    factor_of = block_levels(own_key, dims, split, -0.22, 0.18) if split else 1.0
    entries = jax.random.normal(own_key, dims, jnp.float32) * scale * factor_of
    return jnp.minimum(jnp.maximum(entries, -most), most).astype(held_as)


def setup_inputs(seed: int = 0) -> dict:
    key_of = jax.random.split(jax.random.key(seed), 6)
    residual = gaussian(key_of[0], (TOKENS, D), 1.0, 6.0, ((0, 32),))
    norm_gain = jnp.clip(1.0 + 0.18 * jax.random.normal(key_of[1], (D,), jnp.float32), 0.1, 1.9)
    gate_weight = gaussian(key_of[2], (D, FF), D ** -0.5, 0.125, ((1, 4),))
    up_weight = gaussian(key_of[3], (D, FF), D ** -0.5, 0.125, ((1, 4),))
    hidden_grad = gaussian(key_of[4], (TOKENS, FF), 1.0, 6.0, ((0, 8), (1, 4)))
    return {"residual": residual, "norm_gain": norm_gain, "gate_weight": gate_weight, "up_weight": up_weight, "hidden_grad": hidden_grad}


EPSILON = 1e-05

def normalize(residual):
    values = residual.astype(jnp.float32)
    inverse = lax.rsqrt(lax.optimization_barrier(jnp.mean(values * values, axis=-1, keepdims=True)) + EPSILON)
    return (values * inverse, inverse)

def reference(residual, norm_gain, gate_weight, up_weight, hidden_grad):
    scaled, inverse = normalize(residual)
    normed = (scaled * norm_gain).astype(jnp.bfloat16)
    factor = 1.0 / math.sqrt(TOKENS)
    block = FF // N_TENSOR
    gate_blocks = gate_weight.astype(jnp.float32).reshape(D, N_TENSOR, block)
    up_blocks = up_weight.astype(jnp.float32).reshape(D, N_TENSOR, block)
    normed_groups = normed.reshape(N_DP, ROWS, D)
    upstream_groups = hidden_grad.reshape(N_DP, ROWS, FF)

    def group_step(carry, pieces):
        gate_total, up_total = carry
        normed_rows, upstream_rows = pieces
        gate_value = jnp.dot(normed_rows, gate_weight, preferred_element_type=jnp.float32)
        up_value = jnp.dot(normed_rows, up_weight, preferred_element_type=jnp.float32)
        sigmoid_gate = jax.nn.sigmoid(gate_value)
        upstream = upstream_rows.astype(jnp.float32)
        up_grad = (upstream * gate_value * sigmoid_gate).astype(jnp.bfloat16)
        gate_grad = (upstream * up_value * sigmoid_gate * (1.0 + gate_value * (1.0 - sigmoid_gate))).astype(jnp.bfloat16)
        partial_value = jnp.einsum('rkf,dkf->krd', gate_grad.astype(jnp.float32).reshape(ROWS, N_TENSOR, block), gate_blocks)
        partial_value = partial_value + jnp.einsum('rkf,dkf->krd', up_grad.astype(jnp.float32).reshape(ROWS, N_TENSOR, block), up_blocks)
        normed_grad = lax.optimization_barrier(jnp.sum(lax.optimization_barrier(partial_value.astype(jnp.bfloat16)).astype(jnp.float32), axis=0))
        gate_part = jnp.dot(normed_rows.T, gate_grad, preferred_element_type=jnp.float32) * factor
        up_part = jnp.dot(normed_rows.T, up_grad, preferred_element_type=jnp.float32) * factor
        gate_total = gate_total + lax.optimization_barrier(gate_part.astype(jnp.bfloat16)).astype(jnp.float32)
        up_total = up_total + lax.optimization_barrier(up_part.astype(jnp.bfloat16)).astype(jnp.float32)
        return ((gate_total, up_total), normed_grad)
    zeros = jnp.zeros((D, FF), jnp.float32)
    (gate_total, up_total), normed_grad = lax.scan(group_step, (zeros, zeros), (normed_groups, upstream_groups))
    normed_grad = normed_grad.reshape(TOKENS, D)
    weighted = normed_grad * norm_gain
    residual_grad = ((weighted - scaled * lax.optimization_barrier(jnp.mean(weighted * scaled, axis=-1, keepdims=True))) * inverse).astype(jnp.bfloat16)
    return (residual_grad, gate_total.astype(jnp.bfloat16), up_total.astype(jnp.bfloat16))
```

```python
import jax
import jax.numpy as jnp
from jax import lax
from jax.sharding import PartitionSpec as P

EPSILON = 1e-05


def normalize(residual):
    values = residual.astype(jnp.float32)
    inverse = lax.rsqrt(jnp.mean(values * values, axis=-1, keepdims=True) + EPSILON)
    return (values * inverse, inverse)


def contract_last(left, right):
    return lax.dot_general(
        left, right, (((1,), (1,)), ((), ())), preferred_element_type=jnp.float32
    )


def contract_first(left, right):
    return lax.dot_general(
        left, right, (((0,), (0,)), ((), ())), preferred_element_type=jnp.float32
    )


def gate_grads(normed, gate_weight, up_weight, hidden_grad):
    gate_value = jnp.dot(normed, gate_weight, preferred_element_type=jnp.float32)
    up_value = jnp.dot(normed, up_weight, preferred_element_type=jnp.float32)
    sigmoid_gate = jax.nn.sigmoid(gate_value)
    upstream = hidden_grad.astype(jnp.float32)
    up_grad = (upstream * gate_value * sigmoid_gate).astype(jnp.bfloat16)
    gate_grad = (
        upstream * up_value * sigmoid_gate * (1.0 + gate_value * (1.0 - sigmoid_gate))
    ).astype(jnp.bfloat16)
    return gate_grad, up_grad


def shards(residual, norm_gain, gate_weight, up_weight, hidden_grad):
    rows = hidden_grad.shape[0]
    depth = residual.shape[1] // lax.axis_size("dp")
    me = lax.axis_index("dp")
    whole = lax.all_gather(residual, ("dp", "tensor"), axis=0, tiled=True)
    upstream = lax.all_gather(hidden_grad, "dp", axis=0, tiled=True)
    scaled, inverse = normalize(residual)
    own_rows = lax.dynamic_slice_in_dim(whole, me * rows, rows, 0)
    own_normed = (normalize(own_rows)[0] * norm_gain).astype(jnp.bfloat16)
    gate_grad, up_grad = gate_grads(own_normed, gate_weight, up_weight, hidden_grad)
    normed_grad = lax.psum_scatter(
        (contract_last(gate_grad, gate_weight) + contract_last(up_grad, up_weight)).astype(
            jnp.bfloat16
        ),
        "tensor",
        scatter_dimension=0,
        tiled=True,
    ).astype(jnp.float32)
    weighted = normed_grad * norm_gain
    residual_grad = (
        (weighted - scaled * jnp.mean(weighted * scaled, axis=-1, keepdims=True)) * inverse
    ).astype(jnp.bfloat16)
    factor = float(whole.shape[0]) ** (-0.5)
    normed = (normalize(whole)[0] * norm_gain).astype(jnp.bfloat16)
    gate_all, up_all = gate_grads(normed, gate_weight, up_weight, upstream)
    mine = lax.dynamic_slice_in_dim(normed, me * depth, depth, 1)
    gate_total = contract_first(mine, gate_all) * factor
    up_total = contract_first(mine, up_all) * factor
    return (residual_grad, gate_total.astype(jnp.bfloat16), up_total.astype(jnp.bfloat16))


def solution(mesh):
    return jax.shard_map(
        shards,
        mesh=mesh,
        in_specs=(
            P(("dp", "tensor"), None),
            P(),
            P(None, "tensor"),
            P(None, "tensor"),
            P("dp", "tensor"),
        ),
        out_specs=(P(("dp", "tensor"), None), P("dp", "tensor"), P("dp", "tensor")),
        check_vma=False,
    )
```

```python
import jax
import jax.numpy as jnp
from jax import lax
from jax.experimental import pallas as pl
from jax.experimental.pallas import tpu as pltpu
from jax.sharding import PartitionSpec as P

EPSILON = 1e-05


def normalize(residual):
    values = residual.astype(jnp.float32)
    inverse = lax.rsqrt(jnp.mean(values * values, axis=-1, keepdims=True) + EPSILON)
    return (values * inverse, inverse)


def contract_last(left, right):
    return lax.dot_general(
        left, right, (((1,), (1,)), ((), ())), preferred_element_type=jnp.float32
    )


def contract_first(left, right):
    return lax.dot_general(
        left, right, (((0,), (0,)), ((), ())), preferred_element_type=jnp.float32
    )


def gate_grads(normed, gate_weight, up_weight, hidden_grad):
    gate_value = jnp.dot(normed, gate_weight, preferred_element_type=jnp.float32)
    up_value = jnp.dot(normed, up_weight, preferred_element_type=jnp.float32)
    sigmoid_gate = jax.nn.sigmoid(gate_value)
    upstream = hidden_grad.astype(jnp.float32)
    up_grad = (upstream * gate_value * sigmoid_gate).astype(jnp.bfloat16)
    gate_grad = (
        upstream * up_value * sigmoid_gate * (1.0 + gate_value * (1.0 - sigmoid_gate))
    ).astype(jnp.bfloat16)
    return gate_grad, up_grad


def shards(residual, norm_gain, gate_weight, up_weight, hidden_grad):
    rows = hidden_grad.shape[0]
    depth = residual.shape[1] // lax.axis_size("dp")
    me = lax.axis_index("dp")
    whole = lax.all_gather(residual, ("dp", "tensor"), axis=0, tiled=True)
    upstream = lax.all_gather(hidden_grad, "dp", axis=0, tiled=True)
    scaled, inverse = normalize(residual)
    own_rows = lax.dynamic_slice_in_dim(whole, me * rows, rows, 0)
    own_normed = (normalize(own_rows)[0] * norm_gain).astype(jnp.bfloat16)
    gate_grad, up_grad = gate_grads(own_normed, gate_weight, up_weight, hidden_grad)
    normed_grad = lax.psum_scatter(
        (contract_last(gate_grad, gate_weight) + contract_last(up_grad, up_weight)).astype(
            jnp.bfloat16
        ),
        "tensor",
        scatter_dimension=0,
        tiled=True,
    ).astype(jnp.float32)
    weighted = normed_grad * norm_gain
    residual_grad = (
        (weighted - scaled * jnp.mean(weighted * scaled, axis=-1, keepdims=True)) * inverse
    ).astype(jnp.bfloat16)
    factor = float(whole.shape[0]) ** (-0.5)
    normed = (normalize(whole)[0] * norm_gain).astype(jnp.bfloat16)
    gate_all, up_all = gate_grads(normed, gate_weight, up_weight, upstream)
    mine = lax.dynamic_slice_in_dim(normed, me * depth, depth, 1)
    gate_total = contract_first(mine, gate_all) * factor
    up_total = contract_first(mine, up_all) * factor
    return (residual_grad, gate_total.astype(jnp.bfloat16), up_total.astype(jnp.bfloat16))


MESH = pl.DeviceIdType.MESH
UP, DOWN, ACROSS = 0, 1, 2
TILE = 256


def fused_kernel(
    res_ref, hid_ref, gain_ref, wg_hbm, wu_hbm,
    dres_ref, dwg_ref, dwu_ref,
    wg, wu, res, hid, normed, normed_t, gg, ug, accg, accu, part, parts,
    wsem, lsem, dsend, drecv, msend, mrecv, psend, precv,
):
    me, t = lax.axis_index("dp"), lax.axis_index("tensor")
    z, y = me // 2, me % 2
    rows, wide = hid_ref.shape
    slice_rows, features = res_ref.shape
    depth = dwg_ref.shape[0]
    half = rows // 2
    tokens = res.shape[0]
    factor = float(tokens) ** (-0.5)
    last_z = tokens // rows // 2 - 1
    n_tiles = wide // TILE
    other = me + 1 - 2 * y
    dest = {UP: me + 2, DOWN: me - 2, ACROSS: other}
    order = [
        z,
        jnp.where(z == 0, 1, z - 1),
        jnp.where(z < 2, 2, jnp.where(z == 2, 3, 1)),
        jnp.where(z < 2, 3, 0),
    ]

    def place(g, p):
        if p == 0:
            start = pl.multiple_of(g * rows + t * slice_rows, slice_rows)
            return res.at[pl.ds(start, slice_rows)]
        start = pl.multiple_of(g * rows + (p - 1) * half, half)
        return hid.at[pl.ds(start, half)]

    def route(g, p, kind, own=False):
        dst = place(g, p)
        src = dst
        if own:
            src = res_ref if p == 0 else hid_ref.at[pl.ds((p - 1) * half, half)]
        return pltpu.make_async_remote_copy(
            src_ref=src, dst_ref=dst,
            send_sem=dsend.at[g, p, kind], recv_sem=drecv.at[g, p],
            device_id=(dest[kind], t), device_id_type=MESH,
        )

    def mate(g, k, own=False):
        dst = place(g, 0)
        return pltpu.make_async_remote_copy(
            src_ref=res_ref if own else dst, dst_ref=dst,
            send_sem=msend.at[g, k - 1], recv_sem=mrecv.at[g, k - 1],
            device_id=(me, lax.rem(t + k, 4)), device_id_type=MESH,
        )

    def mates_start(g, own=False):
        for k in (1, 2, 3):
            mate(g, k, own).start()

    def mates_wait(g):
        for k in (1, 2, 3):
            start = pl.multiple_of(g * rows + lax.rem(t + 4 - k, 4) * slice_rows, slice_rows)
            pltpu.make_async_remote_copy(
                src_ref=res.at[pl.ds(start, slice_rows)],
                dst_ref=res.at[pl.ds(start, slice_rows)],
                send_sem=msend.at[g, k - 1], recv_sem=mrecv.at[g, k - 1],
                device_id=(me, lax.rem(t + k, 4)), device_id_type=MESH,
            ).wait_recv()

    def directions(j):
        if j == 0:
            return ((UP, z < last_z), (DOWN, z > 0))
        below = order[j] < z
        return (
            (UP, jnp.logical_and(below, z < last_z)),
            (DOWN, jnp.logical_and(jnp.logical_not(below), z > 0)),
        )

    def send(j, p):
        g = order[j] * 2 + y
        for kind, needed in directions(j):
            @pl.when(needed)
            def _():
                route(g, p, kind, j == 0).start()
        route(g, p, ACROSS, j == 0).start()
        if p == 0 and j > 0:
            mates_start(g)

    def forward(j, p):
        route(order[j] * 2 + y, p, ACROSS).wait_recv()
        send(j, p)

    def from_across(j, p):
        g = order[j] * 2 + 1 - y
        route(g, p, ACROSS).wait_recv()
        if p == 0:
            mates_start(g)

    def norm_rows(zz, r0, count):
        def body(i, carry):
            at = pl.multiple_of(zz * 2 * rows + r0 + i * 32, 32)
            values = res[pl.ds(at, 32), :].astype(jnp.float32)
            inverse = lax.rsqrt(jnp.mean(values * values, axis=-1, keepdims=True) + EPSILON)
            to = pl.multiple_of(r0 + i * 32, 32)
            normed[pl.ds(to, 32), :] = (values * inverse * gain_ref[...]).astype(jnp.bfloat16)
            return carry
        lax.fori_loop(0, count // 32, body, 0)

    def transpose_own():
        columns = pl.ds(pl.multiple_of(me * depth, depth), depth)
        normed_t[...] = normed[:, columns].astype(jnp.float32).T.astype(jnp.bfloat16)

    def tiles(zz, r0, count, lo, hi, weigh=None):
        def body(n, carry):
            columns = pl.ds(pl.multiple_of(n * TILE, TILE), TILE)
            there = pl.ds(pl.multiple_of(r0, rows), count)
            left = normed[there, :]
            gate = jnp.dot(left, wg[:, columns], preferred_element_type=jnp.float32)
            up = jnp.dot(left, wu[:, columns], preferred_element_type=jnp.float32)
            at = pl.ds(pl.multiple_of(zz * 2 * rows + r0, rows), count)
            upstream = hid[at, columns].astype(jnp.float32)
            sig = 0.5 * jnp.tanh(0.5 * gate) + 0.5
            scaled_up = upstream * sig
            ug[there, columns] = (scaled_up * gate).astype(jnp.bfloat16)
            gg[there, columns] = (scaled_up * up * (1.0 + gate * (1.0 - sig))).astype(jnp.bfloat16)
            if weigh is not None:
                for acc, grad, out in ((accg, gg, dwg_ref), (accu, ug, dwu_ref)):
                    term = jnp.dot(normed_t[...], grad[:, columns], preferred_element_type=jnp.float32)
                    if weigh == "first":
                        acc[:, columns] = term
                    elif weigh == "more":
                        acc[:, columns] += term
                    else:
                        out[:, columns] = ((acc[:, columns] + term) * factor).astype(out.dtype)
            return carry
        lax.fori_loop(lo, hi, body, 0)

    def part_copy(k):
        to = lax.rem(t + k, 4)
        start = pl.multiple_of(to * slice_rows, slice_rows)
        return pltpu.make_async_remote_copy(
            src_ref=part.at[pl.ds(start, slice_rows)], dst_ref=parts.at[k - 1],
            send_sem=psend.at[k - 1], recv_sem=precv.at[k - 1],
            device_id=(me, to), device_id_type=MESH,
        )

    def back():
        there = pl.ds(pl.multiple_of(y * rows, rows), rows)
        def body(n, carry):
            at = pl.ds(pl.multiple_of(n * TILE, TILE), TILE)
            dims = (((1,), (1,)), ((), ()))
            total = lax.dot_general(
                gg[there, :], wg[at, :], dims, preferred_element_type=jnp.float32
            ) + lax.dot_general(
                ug[there, :], wu[at, :], dims, preferred_element_type=jnp.float32
            )
            part[:, at] = total.astype(jnp.bfloat16)
            return carry
        lax.fori_loop(0, features // TILE, body, 0)
        for k in (1, 2, 3):
            part_copy(k).start()

    def finish_residual():
        for k in (1, 2, 3):
            part_copy(k).wait_recv()
        own = part[pl.ds(pl.multiple_of(t * slice_rows, slice_rows), slice_rows), :]
        total = own.astype(jnp.float32)
        for k in (0, 1, 2):
            total += parts[k].astype(jnp.float32)
        values = res_ref[...].astype(jnp.float32)
        inverse = lax.rsqrt(jnp.mean(values * values, axis=-1, keepdims=True) + EPSILON)
        scaled = values * inverse
        weighted = total * gain_ref[...]
        mean = jnp.mean(weighted * scaled, axis=-1, keepdims=True)
        dres_ref[...] = ((weighted - scaled * mean) * inverse).astype(dres_ref.dtype)

    weights = [
        pltpu.make_async_copy(wg_hbm, wg, wsem.at[0]),
        pltpu.make_async_copy(wu_hbm, wu, wsem.at[1]),
    ]
    local = [
        pltpu.make_async_copy(
            res_ref, place(me, 0), lsem.at[0]
        ),
        pltpu.make_async_copy(
            hid_ref, hid.at[pl.ds(pl.multiple_of(me * rows, rows), rows)], lsem.at[1]
        ),
    ]
    for copy in weights + local:
        copy.start()

    barrier = pltpu.get_barrier_semaphore()
    for kind, there in directions(0):
        @pl.when(there)
        def _():
            pl.semaphore_signal(barrier, inc=1, device_id=(dest[kind], t), device_id_type=MESH)
    pl.semaphore_signal(barrier, inc=1, device_id=(other, t), device_id_type=MESH)
    for k in (1, 2, 3):
        pl.semaphore_signal(
            barrier, inc=1, device_id=(me, lax.rem(t + k, 4)), device_id_type=MESH
        )
    pl.semaphore_wait(
        barrier, 4 + jnp.where(z > 0, 1, 0) + jnp.where(z < last_z, 1, 0)
    )

    mates_start(me, own=True)
    for p in (0, 1, 2):
        send(0, p)
    for copy in local:
        copy.wait()
    mates_wait(me)
    forward(1, 0)
    norm_rows(z, y * rows, rows)
    for copy in weights:
        copy.wait()
    split = n_tiles // 2 + 1
    tiles(z, y * rows, rows, 0, split)
    from_across(0, 0)
    forward(1, 1)
    tiles(z, y * rows, rows, split, n_tiles)
    forward(1, 2)
    back()
    from_across(0, 1)
    from_across(0, 2)
    forward(2, 0)
    mates_wait(other)
    norm_rows(z, (1 - y) * rows, rows)
    transpose_own()
    tiles(z, (1 - y) * rows, rows, 0, split, "first")
    from_across(1, 0)
    forward(2, 1)
    tiles(z, (1 - y) * rows, rows, split, n_tiles, "first")
    forward(2, 2)

    for j in (1, 2, 3):
        zz = order[j]
        if j == 2:
            finish_residual()
        from_across(j, 1)
        if j == 1:
            from_across(2, 0)
        from_across(j, 2)
        mates_wait(zz * 2)
        mates_wait(zz * 2 + 1)
        norm_rows(zz, 0, 2 * rows)
        transpose_own()
        weigh = "last" if j == 3 else "more"
        if j == 1:
            tiles(zz, 0, 2 * rows, 0, 3, weigh)
            forward(3, 0)
            tiles(zz, 0, 2 * rows, 3, 5, weigh)
            forward(3, 1)
            tiles(zz, 0, 2 * rows, 5, n_tiles, weigh)
            forward(3, 2)
            from_across(3, 0)
        else:
            tiles(zz, 0, 2 * rows, 0, n_tiles, weigh)

    for j in range(4):
        g = order[j] * 2 + y
        for p in (0, 1, 2):
            for kind, needed in directions(j):
                @pl.when(needed)
                def _():
                    route(g, p, kind, j == 0).wait_send()
            route(g, p, ACROSS, j == 0).wait_send()
        for k in (1, 2, 3):
            mate(g, k, j == 0).wait_send()
            mate(order[j] * 2 + 1 - y, k).wait_send()
    for k in (1, 2, 3):
        part_copy(k).wait_send()


def fused_shards(residual, norm_gain, gate_weight, up_weight, hidden_grad):
    slice_rows, features = residual.shape
    rows, wide = hidden_grad.shape
    n_dp = lax.axis_size("dp")
    depth = features // n_dp
    vmem = pl.BlockSpec(memory_space=pltpu.VMEM)
    hbm = pl.BlockSpec(memory_space=pl.ANY)
    low, high = jnp.bfloat16, jnp.float32
    dma = pltpu.SemaphoreType.DMA
    return pl.pallas_call(
        fused_kernel,
        out_shape=(
            jax.ShapeDtypeStruct((slice_rows, features), low),
            jax.ShapeDtypeStruct((depth, wide), low),
            jax.ShapeDtypeStruct((depth, wide), low),
        ),
        in_specs=[vmem, vmem, vmem, hbm, hbm],
        out_specs=(vmem, vmem, vmem),
        scratch_shapes=[
            pltpu.VMEM((features, wide), low),
            pltpu.VMEM((features, wide), low),
            pltpu.VMEM((n_dp * rows, features), low),
            pltpu.VMEM((n_dp * rows, wide), low),
            pltpu.VMEM((2 * rows, features), low),
            pltpu.VMEM((depth, 2 * rows), low),
            pltpu.VMEM((2 * rows, wide), low),
            pltpu.VMEM((2 * rows, wide), low),
            pltpu.VMEM((depth, wide), high),
            pltpu.VMEM((depth, wide), high),
            pltpu.VMEM((rows, features), low),
            pltpu.VMEM((3, slice_rows, features), low),
            dma((2,)),
            dma((2,)),
            dma((n_dp, 3, 3)),
            dma((n_dp, 3)),
            dma((n_dp, 3)),
            dma((n_dp, 3)),
            dma((3,)),
            dma((3,)),
        ],
        compiler_params=pltpu.CompilerParams(
            collective_id=0, has_side_effects=True, vmem_limit_bytes=52 * 1024 * 1024
        ),
    )(residual, hidden_grad, norm_gain.reshape(1, features), gate_weight, up_weight)


def solution(mesh):
    fits = mesh.shape["dp"] == 8 and mesh.shape["tensor"] == 4
    return jax.shard_map(
        fused_shards if fits else shards,
        mesh=mesh,
        in_specs=(
            P(("dp", "tensor"), None),
            P(),
            P(None, "tensor"),
            P(None, "tensor"),
            P("dp", "tensor"),
        ),
        out_specs=(P(("dp", "tensor"), None), P("dp", "tensor"), P("dp", "tensor")),
        check_vma=False,
    )
```

```python
import jax
import jax.numpy as jnp
from jax import lax
from jax.experimental import pallas as pl
from jax.experimental.pallas import tpu as pltpu
from jax.sharding import PartitionSpec as P

EPSILON = 1e-05


def normalize(residual):
    values = residual.astype(jnp.float32)
    inverse = lax.rsqrt(jnp.mean(values * values, axis=-1, keepdims=True) + EPSILON)
    return (values * inverse, inverse)


def contract_last(left, right):
    return lax.dot_general(
        left, right, (((1,), (1,)), ((), ())), preferred_element_type=jnp.float32
    )


def contract_first(left, right):
    return lax.dot_general(
        left, right, (((0,), (0,)), ((), ())), preferred_element_type=jnp.float32
    )


def gate_grads(normed, gate_weight, up_weight, hidden_grad):
    gate_value = jnp.dot(normed, gate_weight, preferred_element_type=jnp.float32)
    up_value = jnp.dot(normed, up_weight, preferred_element_type=jnp.float32)
    sigmoid_gate = jax.nn.sigmoid(gate_value)
    upstream = hidden_grad.astype(jnp.float32)
    up_grad = (upstream * gate_value * sigmoid_gate).astype(jnp.bfloat16)
    gate_grad = (
        upstream * up_value * sigmoid_gate * (1.0 + gate_value * (1.0 - sigmoid_gate))
    ).astype(jnp.bfloat16)
    return gate_grad, up_grad


def shards(residual, norm_gain, gate_weight, up_weight, hidden_grad):
    rows = hidden_grad.shape[0]
    depth = residual.shape[1] // lax.axis_size("dp")
    me = lax.axis_index("dp")
    whole = lax.all_gather(residual, ("dp", "tensor"), axis=0, tiled=True)
    upstream = lax.all_gather(hidden_grad, "dp", axis=0, tiled=True)
    scaled, inverse = normalize(residual)
    own_rows = lax.dynamic_slice_in_dim(whole, me * rows, rows, 0)
    own_normed = (normalize(own_rows)[0] * norm_gain).astype(jnp.bfloat16)
    gate_grad, up_grad = gate_grads(own_normed, gate_weight, up_weight, hidden_grad)
    normed_grad = lax.psum_scatter(
        (contract_last(gate_grad, gate_weight) + contract_last(up_grad, up_weight)).astype(
            jnp.bfloat16
        ),
        "tensor",
        scatter_dimension=0,
        tiled=True,
    ).astype(jnp.float32)
    weighted = normed_grad * norm_gain
    residual_grad = (
        (weighted - scaled * jnp.mean(weighted * scaled, axis=-1, keepdims=True)) * inverse
    ).astype(jnp.bfloat16)
    factor = float(whole.shape[0]) ** (-0.5)
    normed = (normalize(whole)[0] * norm_gain).astype(jnp.bfloat16)
    gate_all, up_all = gate_grads(normed, gate_weight, up_weight, upstream)
    mine = lax.dynamic_slice_in_dim(normed, me * depth, depth, 1)
    gate_total = contract_first(mine, gate_all) * factor
    up_total = contract_first(mine, up_all) * factor
    return (residual_grad, gate_total.astype(jnp.bfloat16), up_total.astype(jnp.bfloat16))


MESH = pl.DeviceIdType.MESH
UP, DOWN, ACROSS = 0, 1, 2
TILE = 256


def fused_kernel(
    res_ref, hid_ref, gain_hbm, wg_hbm, wu_hbm,
    dres_ref, dwg_ref, dwu_ref,
    gain_ref, silu, slope, wg, wu, res, hid, normed, normed_t, gg, ug, accg, accu, part, parts,
    wsem, lsem, dsend, drecv, msend, mrecv, psend, precv,
):
    me, t = lax.axis_index("dp"), lax.axis_index("tensor")
    z, y = me // 2, me % 2
    rows, wide = hid_ref.shape
    slice_rows, features = res_ref.shape
    depth = dwg_ref.shape[0]
    half = rows // 2
    tokens = res.shape[0]
    last_z = tokens // rows // 2 - 1
    n_tiles = wide // TILE
    other = me + 1 - 2 * y
    dest = {UP: me + 2, DOWN: me - 2, ACROSS: other}
    order = [
        z,
        jnp.where(z == 0, 1, z - 1),
        jnp.where(z < 2, 2, jnp.where(z == 2, 3, 1)),
        jnp.where(z < 2, 3, 0),
    ]

    def place(g, p):
        if p == 0:
            start = pl.multiple_of(g * rows + t * slice_rows, slice_rows)
            return res.at[pl.ds(start, slice_rows)]
        start = pl.multiple_of(g * rows + (p - 1) * half, half)
        return hid.at[pl.ds(start, half)]

    def route(g, p, kind, own=False):
        dst = place(g, p)
        src = dst
        if own:
            src = res_ref if p == 0 else hid_ref.at[pl.ds((p - 1) * half, half)]
        return pltpu.make_async_remote_copy(
            src_ref=src, dst_ref=dst,
            send_sem=dsend.at[g, p, kind], recv_sem=drecv.at[g, p],
            device_id=(dest[kind], t), device_id_type=MESH,
        )

    def mate(g, k, own=False):
        dst = place(g, 0)
        return pltpu.make_async_remote_copy(
            src_ref=res_ref if own else dst, dst_ref=dst,
            send_sem=msend.at[g, k - 1], recv_sem=mrecv.at[g, k - 1],
            device_id=(me, lax.rem(t + k, 4)), device_id_type=MESH,
        )

    def mates_start(g, own=False):
        for k in (1, 2, 3):
            mate(g, k, own).start()

    def mates_wait(g):
        for k in (1, 2, 3):
            start = pl.multiple_of(g * rows + lax.rem(t + 4 - k, 4) * slice_rows, slice_rows)
            pltpu.make_async_remote_copy(
                src_ref=res.at[pl.ds(start, slice_rows)],
                dst_ref=res.at[pl.ds(start, slice_rows)],
                send_sem=msend.at[g, k - 1], recv_sem=mrecv.at[g, k - 1],
                device_id=(me, lax.rem(t + k, 4)), device_id_type=MESH,
            ).wait_recv()

    def directions(j):
        if j == 0:
            return ((UP, z < last_z), (DOWN, z > 0))
        below = order[j] < z
        return (
            (UP, jnp.logical_and(below, z < last_z)),
            (DOWN, jnp.logical_and(jnp.logical_not(below), z > 0)),
        )

    def send(j, p):
        g = order[j] * 2 + y
        for kind, needed in directions(j):
            @pl.when(needed)
            def _():
                route(g, p, kind, j == 0).start()
        route(g, p, ACROSS, j == 0).start()
        if p == 0 and j > 0:
            mates_start(g)

    def forward(j, p):
        route(order[j] * 2 + y, p, ACROSS).wait_recv()
        send(j, p)

    def from_across(j, p):
        g = order[j] * 2 + 1 - y
        route(g, p, ACROSS).wait_recv()
        if p == 0:
            mates_start(g)

    def norm_rows(zz, r0, count):
        def body(i, carry):
            at = pl.multiple_of(zz * 2 * rows + r0 + i * 32, 32)
            values = res[pl.ds(at, 32), :].astype(jnp.float32)
            inverse = lax.rsqrt(jnp.mean(values * values, axis=-1, keepdims=True) + EPSILON)
            to = pl.multiple_of(r0 + i * 32, 32)
            normed[pl.ds(to, 32), :] = (values * inverse * gain_ref[...]).astype(jnp.bfloat16)
            return carry
        lax.fori_loop(0, count // 32, body, 0)

    def transpose_own():
        columns = pl.ds(pl.multiple_of(me * depth, depth), depth)
        normed_t[...] = normed[:, columns].astype(jnp.float32).T.astype(jnp.bfloat16)

    def factors(zz, r0, count, lo, hi):
        def body(n, carry):
            columns = pl.ds(pl.multiple_of(n * TILE, TILE), TILE)
            there = pl.ds(pl.multiple_of(r0, rows), count)
            left = normed[there, :]
            gate = jnp.dot(left, wg[:, columns], preferred_element_type=jnp.float32)
            up = jnp.dot(left, wu[:, columns], preferred_element_type=jnp.float32)
            sig = 0.5 * jnp.tanh(0.5 * gate) + 0.5
            silu[there, columns] = gate * sig
            slope[there, columns] = up * sig * (1.0 + gate * (1.0 - sig))
            return carry
        lax.fori_loop(lo, hi, body, 0)

    def weigh_tiles(zz, r0, count, weigh):
        def body(n, carry):
            columns = pl.ds(pl.multiple_of(n * TILE, TILE), TILE)
            there = pl.ds(pl.multiple_of(r0, rows), count)
            at = pl.ds(pl.multiple_of(zz * 2 * rows + r0, rows), count)
            upstream = hid[at, columns].astype(jnp.float32)
            ug[there, columns] = (upstream * silu[there, columns]).astype(jnp.bfloat16)
            gg[there, columns] = (upstream * slope[there, columns]).astype(jnp.bfloat16)
            if weigh is not None:
                for acc, grad, out in ((accg, gg, dwg_ref), (accu, ug, dwu_ref)):
                    term = jnp.dot(normed_t[...], grad[:, columns], preferred_element_type=jnp.float32)
                    if weigh == "first":
                        acc[:, columns] = term
                    elif weigh == "more":
                        acc[:, columns] += term
                    else:
                        out[:, columns] = (acc[:, columns] + term).astype(out.dtype)
            return carry
        lax.fori_loop(0, n_tiles, body, 0)

    def part_copy(k):
        to = lax.rem(t + k, 4)
        start = pl.multiple_of(to * slice_rows, slice_rows)
        return pltpu.make_async_remote_copy(
            src_ref=part.at[pl.ds(start, slice_rows)], dst_ref=parts.at[k - 1],
            send_sem=psend.at[k - 1], recv_sem=precv.at[k - 1],
            device_id=(me, to), device_id_type=MESH,
        )

    def back():
        there = pl.ds(pl.multiple_of(y * rows, rows), rows)
        def body(n, carry):
            at = pl.ds(pl.multiple_of(n * TILE, TILE), TILE)
            dims = (((1,), (1,)), ((), ()))
            total = lax.dot_general(
                gg[there, :], wg[at, :], dims, preferred_element_type=jnp.float32
            ) + lax.dot_general(
                ug[there, :], wu[at, :], dims, preferred_element_type=jnp.float32
            )
            part[:, at] = total.astype(jnp.bfloat16)
            return carry
        lax.fori_loop(0, features // TILE, body, 0)
        for k in (1, 2, 3):
            part_copy(k).start()

    def finish_residual():
        for k in (1, 2, 3):
            part_copy(k).wait_recv()
        own = part[pl.ds(pl.multiple_of(t * slice_rows, slice_rows), slice_rows), :]
        total = own.astype(jnp.float32)
        for k in (0, 1, 2):
            total += parts[k].astype(jnp.float32)
        start = pl.multiple_of(me * rows + t * slice_rows, slice_rows)
        values = res[pl.ds(start, slice_rows), :].astype(jnp.float32)
        inverse = lax.rsqrt(jnp.mean(values * values, axis=-1, keepdims=True) + EPSILON)
        scaled = values * inverse
        weighted = total * gain_ref[...]
        mean = jnp.mean(weighted * scaled, axis=-1, keepdims=True)
        dres_ref[...] = ((weighted - scaled * mean) * inverse).astype(dres_ref.dtype)

    weights = [
        pltpu.make_async_copy(wg_hbm, wg, wsem.at[0]),
        pltpu.make_async_copy(wu_hbm, wu, wsem.at[1]),
    ]
    local = [
        pltpu.make_async_copy(
            res_ref, place(me, 0), lsem.at[0]
        ),
        pltpu.make_async_copy(
            hid_ref, hid.at[pl.ds(pl.multiple_of(me * rows, rows), rows)], lsem.at[1]
        ),
        pltpu.make_async_copy(gain_hbm, gain_ref, lsem.at[2]),
    ]
    for copy in local + weights:
        copy.start()

    barrier = pltpu.get_barrier_semaphore()
    for kind, there in directions(0):
        @pl.when(there)
        def _():
            pl.semaphore_signal(barrier, inc=1, device_id=(dest[kind], t), device_id_type=MESH)
    pl.semaphore_signal(barrier, inc=1, device_id=(other, t), device_id_type=MESH)
    for k in (1, 2, 3):
        pl.semaphore_signal(
            barrier, inc=1, device_id=(me, lax.rem(t + k, 4)), device_id_type=MESH
        )
    pl.semaphore_wait(
        barrier, 4 + jnp.where(z > 0, 1, 0) + jnp.where(z < last_z, 1, 0)
    )

    own_row, other_row = y * rows, (1 - y) * rows
    mates_start(me, own=True)
    send(0, 0)
    send(0, 1)
    for copy in local:
        copy.wait()
    forward(1, 0)
    from_across(0, 0)
    send(0, 2)
    mates_wait(me)
    norm_rows(z, own_row, rows)
    for copy in weights:
        copy.wait()
    factors(z, own_row, rows, 0, 2)
    forward(2, 0)
    factors(z, own_row, rows, 2, 4)
    forward(3, 0)
    from_across(1, 0)
    factors(z, own_row, rows, 4, n_tiles)
    forward(1, 1)
    weigh_tiles(z, own_row, rows, None)
    forward(1, 2)
    from_across(2, 0)
    back()
    from_across(3, 0)
    mates_wait(other)
    norm_rows(z, other_row, rows)
    factors(z, other_row, rows, 0, 4)
    forward(2, 1)
    factors(z, other_row, rows, 4, n_tiles)
    from_across(0, 1)
    from_across(0, 2)
    transpose_own()
    weigh_tiles(z, other_row, rows, "first")

    for j in (1, 2, 3):
        zz = order[j]
        mates_wait(zz * 2)
        mates_wait(zz * 2 + 1)
        norm_rows(zz, 0, 2 * rows)
        transpose_own()
        factors(zz, 0, 2 * rows, 0, 4)
        if j == 1:
            forward(2, 2)
        if j == 2:
            forward(3, 2)
        factors(zz, 0, 2 * rows, 4, n_tiles)
        if j == 1:
            forward(3, 1)
        if j == 3:
            finish_residual()
        from_across(j, 1)
        from_across(j, 2)
        weigh_tiles(zz, 0, 2 * rows, "last" if j == 3 else "more")

    for j in range(4):
        g = order[j] * 2 + y
        for p in (0, 1, 2):
            for kind, needed in directions(j):
                @pl.when(needed)
                def _():
                    route(g, p, kind, j == 0).wait_send()
            route(g, p, ACROSS, j == 0).wait_send()
        for k in (1, 2, 3):
            mate(g, k, j == 0).wait_send()
            mate(order[j] * 2 + 1 - y, k).wait_send()
    for k in (1, 2, 3):
        part_copy(k).wait_send()


def fused_shards(residual, norm_gain, gate_weight, up_weight, hidden_grad):
    slice_rows, features = residual.shape
    rows, wide = hidden_grad.shape
    n_dp = lax.axis_size("dp")
    depth = features // n_dp
    vmem = pl.BlockSpec(memory_space=pltpu.VMEM)
    hbm = pl.BlockSpec(memory_space=pltpu.HBM)
    low, high = jnp.bfloat16, jnp.float32
    dma = pltpu.SemaphoreType.DMA
    dres, dwg, dwu = pl.pallas_call(
        fused_kernel,
        out_shape=(
            jax.ShapeDtypeStruct((slice_rows, features), low),
            jax.ShapeDtypeStruct((depth, wide), low),
            jax.ShapeDtypeStruct((depth, wide), low),
        ),
        in_specs=[hbm] * 5,
        out_specs=(vmem, vmem, vmem),
        scratch_shapes=[
            pltpu.VMEM((1, features), high),
            pltpu.VMEM((2 * rows, wide), high),
            pltpu.VMEM((2 * rows, wide), high),
            pltpu.VMEM((features, wide), low),
            pltpu.VMEM((features, wide), low),
            pltpu.VMEM((n_dp * rows, features), low),
            pltpu.VMEM((n_dp * rows, wide), low),
            pltpu.VMEM((2 * rows, features), low),
            pltpu.VMEM((depth, 2 * rows), low),
            pltpu.VMEM((2 * rows, wide), low),
            pltpu.VMEM((2 * rows, wide), low),
            pltpu.VMEM((depth, wide), high),
            pltpu.VMEM((depth, wide), high),
            pltpu.VMEM((rows, features), low),
            pltpu.VMEM((3, slice_rows, features), low),
            dma((2,)),
            dma((3,)),
            dma((n_dp, 3, 3)),
            dma((n_dp, 3)),
            dma((n_dp, 3)),
            dma((n_dp, 3)),
            dma((3,)),
            dma((3,)),
        ],
        compiler_params=pltpu.CompilerParams(
            collective_id=0, has_side_effects=True, vmem_limit_bytes=56 * 1024 * 1024
        ),
    )(residual, hidden_grad, norm_gain.reshape(1, features), gate_weight, up_weight)
    factor = float(n_dp * rows) ** (-0.5)
    scale = lambda total: (total.astype(high) * factor).astype(low)
    return dres, scale(dwg), scale(dwu)


def solution(mesh):
    fits = mesh.shape["dp"] == 8 and mesh.shape["tensor"] == 4
    return jax.shard_map(
        fused_shards if fits else shards,
        mesh=mesh,
        in_specs=(
            P(("dp", "tensor"), None),
            P(),
            P(None, "tensor"),
            P(None, "tensor"),
            P("dp", "tensor"),
        ),
        out_specs=(P(("dp", "tensor"), None), P("dp", "tensor"), P("dp", "tensor")),
        check_vma=False,
    )
```

```python
import jax
import jax.numpy as jnp
from jax import lax
from jax.experimental import pallas as pl
from jax.experimental.pallas import tpu as pltpu
from jax.sharding import PartitionSpec as P

EPSILON = 1e-05


def normalize(residual):
    values = residual.astype(jnp.float32)
    inverse = lax.rsqrt(jnp.mean(values * values, axis=-1, keepdims=True) + EPSILON)
    return (values * inverse, inverse)


def contract_last(left, right):
    return lax.dot_general(
        left, right, (((1,), (1,)), ((), ())), preferred_element_type=jnp.float32
    )


def contract_first(left, right):
    return lax.dot_general(
        left, right, (((0,), (0,)), ((), ())), preferred_element_type=jnp.float32
    )


def gate_grads(normed, gate_weight, up_weight, hidden_grad):
    gate_value = jnp.dot(normed, gate_weight, preferred_element_type=jnp.float32)
    up_value = jnp.dot(normed, up_weight, preferred_element_type=jnp.float32)
    sigmoid_gate = jax.nn.sigmoid(gate_value)
    upstream = hidden_grad.astype(jnp.float32)
    up_grad = (upstream * gate_value * sigmoid_gate).astype(jnp.bfloat16)
    gate_grad = (
        upstream * up_value * sigmoid_gate * (1.0 + gate_value * (1.0 - sigmoid_gate))
    ).astype(jnp.bfloat16)
    return gate_grad, up_grad


def shards(residual, norm_gain, gate_weight, up_weight, hidden_grad):
    rows = hidden_grad.shape[0]
    depth = residual.shape[1] // lax.axis_size("dp")
    me = lax.axis_index("dp")
    whole = lax.all_gather(residual, ("dp", "tensor"), axis=0, tiled=True)
    upstream = lax.all_gather(hidden_grad, "dp", axis=0, tiled=True)
    scaled, inverse = normalize(residual)
    own_rows = lax.dynamic_slice_in_dim(whole, me * rows, rows, 0)
    own_normed = (normalize(own_rows)[0] * norm_gain).astype(jnp.bfloat16)
    gate_grad, up_grad = gate_grads(own_normed, gate_weight, up_weight, hidden_grad)
    normed_grad = lax.psum_scatter(
        (contract_last(gate_grad, gate_weight) + contract_last(up_grad, up_weight)).astype(
            jnp.bfloat16
        ),
        "tensor",
        scatter_dimension=0,
        tiled=True,
    ).astype(jnp.float32)
    weighted = normed_grad * norm_gain
    residual_grad = (
        (weighted - scaled * jnp.mean(weighted * scaled, axis=-1, keepdims=True)) * inverse
    ).astype(jnp.bfloat16)
    factor = float(whole.shape[0]) ** (-0.5)
    normed = (normalize(whole)[0] * norm_gain).astype(jnp.bfloat16)
    gate_all, up_all = gate_grads(normed, gate_weight, up_weight, upstream)
    mine = lax.dynamic_slice_in_dim(normed, me * depth, depth, 1)
    gate_total = contract_first(mine, gate_all) * factor
    up_total = contract_first(mine, up_all) * factor
    return (residual_grad, gate_total.astype(jnp.bfloat16), up_total.astype(jnp.bfloat16))


MESH = pl.DeviceIdType.MESH
UP, DOWN, ACROSS = 0, 1, 2
TILE = 256


def fused_kernel(
    res_ref, hid_ref, gain_hbm, wg_hbm, wu_hbm,
    dres_ref, dwg_ref, dwu_ref,
    gain_ref, silu, slope, wg, wu, res, hid, normed, normed_t, gg, ug, accg, accu, part, parts,
    wsem, lsem, dsend, drecv, msend, mrecv, psend, precv,
):
    me, t = lax.axis_index("dp"), lax.axis_index("tensor")
    z, y = me // 2, me % 2
    rows, wide = hid_ref.shape
    slice_rows, features = res_ref.shape
    depth = dwg_ref.shape[0]
    half = rows // 2
    tokens = res.shape[0]
    last_z = tokens // rows // 2 - 1
    n_tiles = wide // TILE
    other = me + 1 - 2 * y
    dest = {UP: me + 2, DOWN: me - 2, ACROSS: other}
    order = [
        z,
        jnp.where(z == 0, 1, z - 1),
        jnp.where(z < 2, 2, jnp.where(z == 2, 3, 1)),
        jnp.where(z < 2, 3, 0),
    ]

    def place(g, p):
        if p == 0:
            start = pl.multiple_of(g * rows + t * slice_rows, slice_rows)
            return res.at[pl.ds(start, slice_rows)]
        start = pl.multiple_of(g * rows + (p - 1) * half, half)
        return hid.at[pl.ds(start, half)]

    def route(g, p, kind, own=False):
        dst = place(g, p)
        src = dst
        if own:
            src = res_ref if p == 0 else hid_ref.at[pl.ds((p - 1) * half, half)]
        return pltpu.make_async_remote_copy(
            src_ref=src, dst_ref=dst,
            send_sem=dsend.at[g, p, kind], recv_sem=drecv.at[g, p],
            device_id=(dest[kind], t), device_id_type=MESH,
        )

    def mate(g, k, own=False):
        dst = place(g, 0)
        return pltpu.make_async_remote_copy(
            src_ref=res_ref if own else dst, dst_ref=dst,
            send_sem=msend.at[g, k - 1], recv_sem=mrecv.at[g, k - 1],
            device_id=(me, lax.rem(t + k, 4)), device_id_type=MESH,
        )

    def mates_start(g, own=False):
        for k in (1, 2, 3):
            mate(g, k, own).start()

    def mates_wait(g):
        for k in (1, 2, 3):
            start = pl.multiple_of(g * rows + lax.rem(t + 4 - k, 4) * slice_rows, slice_rows)
            pltpu.make_async_remote_copy(
                src_ref=res.at[pl.ds(start, slice_rows)],
                dst_ref=res.at[pl.ds(start, slice_rows)],
                send_sem=msend.at[g, k - 1], recv_sem=mrecv.at[g, k - 1],
                device_id=(me, lax.rem(t + k, 4)), device_id_type=MESH,
            ).wait_recv()

    def directions(j):
        if j == 0:
            return ((UP, z < last_z), (DOWN, z > 0))
        below = order[j] < z
        return (
            (UP, jnp.logical_and(below, z < last_z)),
            (DOWN, jnp.logical_and(jnp.logical_not(below), z > 0)),
        )

    def send(j, p):
        g = order[j] * 2 + y
        for kind, needed in directions(j):
            @pl.when(needed)
            def _():
                route(g, p, kind, j == 0).start()
        route(g, p, ACROSS, j == 0).start()
        if p == 0 and j > 0:
            mates_start(g)

    def forward(j, p):
        route(order[j] * 2 + y, p, ACROSS).wait_recv()
        send(j, p)

    def forward_if(needed, j, p):
        @pl.when(needed)
        def _():
            forward(j, p)

    inner = jnp.logical_and(z > 0, z < last_z)
    outer = jnp.logical_not(inner)

    def from_across(j, p):
        g = order[j] * 2 + 1 - y
        route(g, p, ACROSS).wait_recv()
        if p == 0:
            mates_start(g)

    def norm_rows(zz, r0, count):
        def body(i, carry):
            at = pl.multiple_of(zz * 2 * rows + r0 + i * 32, 32)
            values = res[pl.ds(at, 32), :].astype(jnp.float32)
            inverse = lax.rsqrt(jnp.mean(values * values, axis=-1, keepdims=True) + EPSILON)
            to = pl.multiple_of(r0 + i * 32, 32)
            normed[pl.ds(to, 32), :] = (values * inverse * gain_ref[...]).astype(jnp.bfloat16)
            return carry
        lax.fori_loop(0, count // 32, body, 0)

    def transpose_own():
        columns = pl.ds(pl.multiple_of(me * depth, depth), depth)
        normed_t[...] = normed[:, columns].astype(jnp.float32).T.astype(jnp.bfloat16)

    def factors(zz, r0, count, lo, hi):
        def body(n, carry):
            columns = pl.ds(pl.multiple_of(n * TILE, TILE), TILE)
            there = pl.ds(pl.multiple_of(r0, rows), count)
            left = normed[there, :]
            gate = jnp.dot(left, wg[:, columns], preferred_element_type=jnp.float32)
            up = jnp.dot(left, wu[:, columns], preferred_element_type=jnp.float32)
            sig = 0.5 * jnp.tanh(0.5 * gate) + 0.5
            silu[there, columns] = gate * sig
            slope[there, columns] = up * sig * (1.0 + gate * (1.0 - sig))
            return carry
        lax.fori_loop(lo, hi, body, 0, unroll=True)

    def weigh_tiles(zz, r0, count, weigh):
        def body(n, carry):
            columns = pl.ds(pl.multiple_of(n * TILE, TILE), TILE)
            there = pl.ds(pl.multiple_of(r0, rows), count)
            at = pl.ds(pl.multiple_of(zz * 2 * rows + r0, rows), count)
            upstream = hid[at, columns].astype(jnp.float32)
            ug[there, columns] = (upstream * silu[there, columns]).astype(jnp.bfloat16)
            gg[there, columns] = (upstream * slope[there, columns]).astype(jnp.bfloat16)
            if weigh is not None:
                for acc, grad, out in ((accg, gg, dwg_ref), (accu, ug, dwu_ref)):
                    term = jnp.dot(normed_t[...], grad[:, columns], preferred_element_type=jnp.float32)
                    if weigh == "first":
                        acc[:, columns] = term
                    elif weigh == "more":
                        acc[:, columns] += term
                    else:
                        out[:, columns] = (acc[:, columns] + term).astype(out.dtype)
            return carry
        lax.fori_loop(0, n_tiles, body, 0, unroll=True)

    def part_copy(k):
        to = lax.rem(t + k, 4)
        start = pl.multiple_of(to * slice_rows, slice_rows)
        return pltpu.make_async_remote_copy(
            src_ref=part.at[pl.ds(start, slice_rows)], dst_ref=parts.at[k - 1],
            send_sem=psend.at[k - 1], recv_sem=precv.at[k - 1],
            device_id=(me, to), device_id_type=MESH,
        )

    def back():
        there = pl.ds(pl.multiple_of(y * rows, rows), rows)
        def body(n, carry):
            at = pl.ds(pl.multiple_of(n * TILE, TILE), TILE)
            dims = (((1,), (1,)), ((), ()))
            total = lax.dot_general(
                gg[there, :], wg[at, :], dims, preferred_element_type=jnp.float32
            ) + lax.dot_general(
                ug[there, :], wu[at, :], dims, preferred_element_type=jnp.float32
            )
            part[:, at] = total.astype(jnp.bfloat16)
            return carry
        lax.fori_loop(0, features // TILE, body, 0)
        for k in (1, 2, 3):
            part_copy(k).start()

    def finish_residual():
        for k in (1, 2, 3):
            part_copy(k).wait_recv()
        own = part[pl.ds(pl.multiple_of(t * slice_rows, slice_rows), slice_rows), :]
        total = own.astype(jnp.float32)
        for k in (0, 1, 2):
            total += parts[k].astype(jnp.float32)
        start = pl.multiple_of(me * rows + t * slice_rows, slice_rows)
        values = res[pl.ds(start, slice_rows), :].astype(jnp.float32)
        inverse = lax.rsqrt(jnp.mean(values * values, axis=-1, keepdims=True) + EPSILON)
        scaled = values * inverse
        weighted = total * gain_ref[...]
        mean = jnp.mean(weighted * scaled, axis=-1, keepdims=True)
        dres_ref[...] = ((weighted - scaled * mean) * inverse).astype(dres_ref.dtype)

    weights = [
        pltpu.make_async_copy(wg_hbm, wg, wsem.at[0]),
        pltpu.make_async_copy(wu_hbm, wu, wsem.at[1]),
    ]
    local = [
        pltpu.make_async_copy(
            res_ref, place(me, 0), lsem.at[0]
        ),
        pltpu.make_async_copy(
            hid_ref, hid.at[pl.ds(pl.multiple_of(me * rows, rows), rows)], lsem.at[1]
        ),
        pltpu.make_async_copy(gain_hbm, gain_ref, lsem.at[2]),
    ]
    for copy in local + weights:
        copy.start()

    barrier = pltpu.get_barrier_semaphore()
    for kind, there in directions(0):
        @pl.when(there)
        def _():
            pl.semaphore_signal(barrier, inc=1, device_id=(dest[kind], t), device_id_type=MESH)
    pl.semaphore_signal(barrier, inc=1, device_id=(other, t), device_id_type=MESH)
    for k in (1, 2, 3):
        pl.semaphore_signal(
            barrier, inc=1, device_id=(me, lax.rem(t + k, 4)), device_id_type=MESH
        )
    pl.semaphore_wait(
        barrier, 4 + jnp.where(z > 0, 1, 0) + jnp.where(z < last_z, 1, 0)
    )

    own_row, other_row = y * rows, (1 - y) * rows
    mates_start(me, own=True)
    send(0, 0)
    send(0, 1)
    for copy in local:
        copy.wait()
    forward(1, 0)
    from_across(0, 0)
    send(0, 2)
    mates_wait(me)
    norm_rows(z, own_row, rows)
    for copy in weights:
        copy.wait()
    factors(z, own_row, rows, 0, 2)
    forward(2, 0)
    factors(z, own_row, rows, 2, 4)
    forward(3, 0)
    forward(1, 1)
    forward_if(inner, 2, 1)
    from_across(1, 0)
    factors(z, own_row, rows, 4, n_tiles)
    forward(1, 2)
    forward_if(inner, 2, 2)
    from_across(2, 0)
    weigh_tiles(z, own_row, rows, None)
    back()
    from_across(3, 0)
    mates_wait(other)
    norm_rows(z, other_row, rows)
    factors(z, other_row, rows, 0, 4)
    forward_if(outer, 2, 1)
    forward_if(inner, 3, 1)
    factors(z, other_row, rows, 4, n_tiles)
    forward_if(outer, 2, 2)
    forward_if(inner, 3, 2)
    from_across(0, 1)
    from_across(0, 2)
    transpose_own()
    weigh_tiles(z, other_row, rows, "first")

    for j in (1, 2, 3):
        zz = order[j]
        mates_wait(zz * 2)
        mates_wait(zz * 2 + 1)
        norm_rows(zz, 0, 2 * rows)
        transpose_own()
        factors(zz, 0, 2 * rows, 0, 4)
        if j == 1:
            forward_if(outer, 3, 1)
        factors(zz, 0, 2 * rows, 4, n_tiles)
        if j == 1:
            forward_if(outer, 3, 2)
        if j == 3:
            finish_residual()
        from_across(j, 1)
        from_across(j, 2)
        weigh_tiles(zz, 0, 2 * rows, "last" if j == 3 else "more")

    for j in range(4):
        g = order[j] * 2 + y
        for p in (0, 1, 2):
            for kind, needed in directions(j):
                @pl.when(needed)
                def _():
                    route(g, p, kind, j == 0).wait_send()
            route(g, p, ACROSS, j == 0).wait_send()
        for k in (1, 2, 3):
            mate(g, k, j == 0).wait_send()
            mate(order[j] * 2 + 1 - y, k).wait_send()
    for k in (1, 2, 3):
        part_copy(k).wait_send()


def fused_shards(residual, norm_gain, gate_weight, up_weight, hidden_grad):
    slice_rows, features = residual.shape
    rows, wide = hidden_grad.shape
    n_dp = lax.axis_size("dp")
    depth = features // n_dp
    vmem = pl.BlockSpec(memory_space=pltpu.VMEM)
    hbm = pl.BlockSpec(memory_space=pltpu.HBM)
    low, high = jnp.bfloat16, jnp.float32
    dma = pltpu.SemaphoreType.DMA
    dres, dwg, dwu = pl.pallas_call(
        fused_kernel,
        out_shape=(
            jax.ShapeDtypeStruct((slice_rows, features), low),
            jax.ShapeDtypeStruct((depth, wide), low),
            jax.ShapeDtypeStruct((depth, wide), low),
        ),
        in_specs=[hbm] * 5,
        out_specs=(vmem, vmem, vmem),
        scratch_shapes=[
            pltpu.VMEM((1, features), high),
            pltpu.VMEM((2 * rows, wide), high),
            pltpu.VMEM((2 * rows, wide), high),
            pltpu.VMEM((features, wide), low),
            pltpu.VMEM((features, wide), low),
            pltpu.VMEM((n_dp * rows, features), low),
            pltpu.VMEM((n_dp * rows, wide), low),
            pltpu.VMEM((2 * rows, features), low),
            pltpu.VMEM((depth, 2 * rows), low),
            pltpu.VMEM((2 * rows, wide), low),
            pltpu.VMEM((2 * rows, wide), low),
            pltpu.VMEM((depth, wide), high),
            pltpu.VMEM((depth, wide), high),
            pltpu.VMEM((rows, features), low),
            pltpu.VMEM((3, slice_rows, features), low),
            dma((2,)),
            dma((3,)),
            dma((n_dp, 3, 3)),
            dma((n_dp, 3)),
            dma((n_dp, 3)),
            dma((n_dp, 3)),
            dma((3,)),
            dma((3,)),
        ],
        compiler_params=pltpu.CompilerParams(
            collective_id=0, has_side_effects=True, vmem_limit_bytes=44 * 1024 * 1024
        ),
    )(residual, hidden_grad, norm_gain.reshape(1, features), gate_weight, up_weight)
    factor = float(n_dp * rows) ** (-0.5)
    scale = lambda total: (total.astype(high) * factor).astype(low)
    return dres, scale(dwg), scale(dwu)


def solution(mesh):
    fits = mesh.shape["dp"] == 8 and mesh.shape["tensor"] == 4
    return jax.shard_map(
        fused_shards if fits else shards,
        mesh=mesh,
        in_specs=(
            P(("dp", "tensor"), None),
            P(),
            P(None, "tensor"),
            P(None, "tensor"),
            P("dp", "tensor"),
        ),
        out_specs=(P(("dp", "tensor"), None), P("dp", "tensor"), P("dp", "tensor")),
        check_vma=False,
    )
```

```python
import jax
import jax.numpy as jnp
from jax import lax
from jax.experimental import pallas as pl
from jax.experimental.pallas import tpu as pltpu
from jax.sharding import PartitionSpec as P

EPSILON = 1e-05


def normalize(residual):
    values = residual.astype(jnp.float32)
    inverse = lax.rsqrt(jnp.mean(values * values, axis=-1, keepdims=True) + EPSILON)
    return (values * inverse, inverse)


def contract_last(left, right):
    return lax.dot_general(
        left, right, (((1,), (1,)), ((), ())), preferred_element_type=jnp.float32
    )


def contract_first(left, right):
    return lax.dot_general(
        left, right, (((0,), (0,)), ((), ())), preferred_element_type=jnp.float32
    )


def gate_grads(normed, gate_weight, up_weight, hidden_grad):
    gate_value = jnp.dot(normed, gate_weight, preferred_element_type=jnp.float32)
    up_value = jnp.dot(normed, up_weight, preferred_element_type=jnp.float32)
    sigmoid_gate = jax.nn.sigmoid(gate_value)
    upstream = hidden_grad.astype(jnp.float32)
    up_grad = (upstream * gate_value * sigmoid_gate).astype(jnp.bfloat16)
    gate_grad = (
        upstream * up_value * sigmoid_gate * (1.0 + gate_value * (1.0 - sigmoid_gate))
    ).astype(jnp.bfloat16)
    return gate_grad, up_grad


def shards(residual, norm_gain, gate_weight, up_weight, hidden_grad):
    rows = hidden_grad.shape[0]
    depth = residual.shape[1] // lax.axis_size("dp")
    me = lax.axis_index("dp")
    whole = lax.all_gather(residual, ("dp", "tensor"), axis=0, tiled=True)
    upstream = lax.all_gather(hidden_grad, "dp", axis=0, tiled=True)
    scaled, inverse = normalize(residual)
    own_rows = lax.dynamic_slice_in_dim(whole, me * rows, rows, 0)
    own_normed = (normalize(own_rows)[0] * norm_gain).astype(jnp.bfloat16)
    gate_grad, up_grad = gate_grads(own_normed, gate_weight, up_weight, hidden_grad)
    normed_grad = lax.psum_scatter(
        (contract_last(gate_grad, gate_weight) + contract_last(up_grad, up_weight)).astype(
            jnp.bfloat16
        ),
        "tensor",
        scatter_dimension=0,
        tiled=True,
    ).astype(jnp.float32)
    weighted = normed_grad * norm_gain
    residual_grad = (
        (weighted - scaled * jnp.mean(weighted * scaled, axis=-1, keepdims=True)) * inverse
    ).astype(jnp.bfloat16)
    factor = float(whole.shape[0]) ** (-0.5)
    normed = (normalize(whole)[0] * norm_gain).astype(jnp.bfloat16)
    gate_all, up_all = gate_grads(normed, gate_weight, up_weight, upstream)
    mine = lax.dynamic_slice_in_dim(normed, me * depth, depth, 1)
    gate_total = contract_first(mine, gate_all) * factor
    up_total = contract_first(mine, up_all) * factor
    return (residual_grad, gate_total.astype(jnp.bfloat16), up_total.astype(jnp.bfloat16))


MESH = pl.DeviceIdType.MESH
UP, DOWN, ACROSS = 0, 1, 2
TILE = 256


def fused_kernel(
    res_ref, hid_ref, gain_hbm, wg_hbm, wu_hbm,
    dres_ref, dwg_ref, dwu_ref,
    gain_ref, silu, slope, wg, wu, res, hid, normed, normed_t, gg, ug, accg, accu, part, parts,
    wsem, lsem, dsend, drecv, msend, mrecv, psend, precv,
):
    me, t = lax.axis_index("dp"), lax.axis_index("tensor")
    z, y = me // 2, me % 2
    rows, wide = hid_ref.shape
    slice_rows, features = res_ref.shape
    depth = dwg_ref.shape[0]
    half = rows // 2
    tokens = res.shape[0]
    last_z = tokens // rows // 2 - 1
    n_tiles = wide // TILE
    other = me + 1 - 2 * y
    dest = {UP: me + 2, DOWN: me - 2, ACROSS: other}
    order = [
        z,
        jnp.where(z == 0, 1, z - 1),
        jnp.where(z < 2, 2, jnp.where(z == 2, 3, 1)),
        jnp.where(z < 2, 3, 0),
    ]

    def place(g, p):
        if p == 0:
            start = pl.multiple_of(g * rows + t * slice_rows, slice_rows)
            return res.at[pl.ds(start, slice_rows)]
        start = pl.multiple_of(g * rows + (p - 1) * half, half)
        return hid.at[pl.ds(start, half)]

    def route(g, p, kind, own=False):
        dst = place(g, p)
        src = dst
        if own:
            src = res_ref if p == 0 else hid_ref.at[pl.ds((p - 1) * half, half)]
        return pltpu.make_async_remote_copy(
            src_ref=src, dst_ref=dst,
            send_sem=dsend.at[g, p, kind], recv_sem=drecv.at[g, p],
            device_id=(dest[kind], t), device_id_type=MESH,
        )

    def mate(g, k, own=False):
        dst = place(g, 0)
        return pltpu.make_async_remote_copy(
            src_ref=res_ref if own else dst, dst_ref=dst,
            send_sem=msend.at[g, k - 1], recv_sem=mrecv.at[g, k - 1],
            device_id=(me, lax.rem(t + k, 4)), device_id_type=MESH,
        )

    def mates_start(g, own=False):
        for k in (1, 2, 3):
            mate(g, k, own).start()

    def mates_wait(g):
        for k in (1, 2, 3):
            start = pl.multiple_of(g * rows + lax.rem(t + 4 - k, 4) * slice_rows, slice_rows)
            pltpu.make_async_remote_copy(
                src_ref=res.at[pl.ds(start, slice_rows)],
                dst_ref=res.at[pl.ds(start, slice_rows)],
                send_sem=msend.at[g, k - 1], recv_sem=mrecv.at[g, k - 1],
                device_id=(me, lax.rem(t + k, 4)), device_id_type=MESH,
            ).wait_recv()

    def directions(j):
        if j == 0:
            return ((UP, z < last_z), (DOWN, z > 0))
        below = order[j] < z
        return (
            (UP, jnp.logical_and(below, z < last_z)),
            (DOWN, jnp.logical_and(jnp.logical_not(below), z > 0)),
        )

    def by_line(j, p):
        return j == 1 and p == 2

    line = ((UP, z < last_z), (DOWN, z == 1))

    def send(j, p):
        g = order[j] * 2 + y
        for kind, needed in directions(j):
            @pl.when(needed)
            def _():
                route(g, p, kind, j == 0).start()
        if not by_line(j, p):
            route(g, p, ACROSS, j == 0).start()
        if p == 0 and j > 0:
            mates_start(g)

    def forward(j, p):
        route(order[j] * 2 + y, p, ACROSS).wait_recv()
        send(j, p)

    def forward_if(needed, j, p):
        @pl.when(needed)
        def _():
            forward(j, p)

    inner = jnp.logical_and(z > 0, z < last_z)
    outer = jnp.logical_not(inner)

    def from_across(j, p):
        g = order[j] * 2 + 1 - y
        route(g, p, ACROSS).wait_recv()
        if p == 0:
            mates_start(g)
        if (j, p) == (0, 2):
            for kind, needed in line:
                @pl.when(needed)
                def _():
                    route(g, p, kind).start()

    def norm_rows(zz, r0, count):
        def body(i, carry):
            at = pl.multiple_of(zz * 2 * rows + r0 + i * 32, 32)
            values = res[pl.ds(at, 32), :].astype(jnp.float32)
            inverse = lax.rsqrt(jnp.mean(values * values, axis=-1, keepdims=True) + EPSILON)
            to = pl.multiple_of(r0 + i * 32, 32)
            normed[pl.ds(to, 32), :] = (values * inverse * gain_ref[...]).astype(jnp.bfloat16)
            return carry
        lax.fori_loop(0, count // 32, body, 0)

    def transpose_own():
        columns = pl.ds(pl.multiple_of(me * depth, depth), depth)
        normed_t[...] = normed[:, columns].astype(jnp.float32).T.astype(jnp.bfloat16)

    def factors(zz, r0, count, lo, hi):
        def body(n, carry):
            columns = pl.ds(pl.multiple_of(n * TILE, TILE), TILE)
            there = pl.ds(pl.multiple_of(r0, rows), count)
            left = normed[there, :]
            gate = jnp.dot(left, wg[:, columns], preferred_element_type=jnp.float32)
            up = jnp.dot(left, wu[:, columns], preferred_element_type=jnp.float32)
            sig = 0.5 * jnp.tanh(0.5 * gate) + 0.5
            silu[there, columns] = gate * sig
            slope[there, columns] = up * sig * (1.0 + gate * (1.0 - sig))
            return carry
        lax.fori_loop(lo, hi, body, 0, unroll=True)

    def weigh_tiles(zz, r0, count, weigh):
        def body(n, carry):
            columns = pl.ds(pl.multiple_of(n * TILE, TILE), TILE)
            there = pl.ds(pl.multiple_of(r0, rows), count)
            at = pl.ds(pl.multiple_of(zz * 2 * rows + r0, rows), count)
            upstream = hid[at, columns].astype(jnp.float32)
            ug[there, columns] = (upstream * silu[there, columns]).astype(jnp.bfloat16)
            gg[there, columns] = (upstream * slope[there, columns]).astype(jnp.bfloat16)
            if weigh is not None:
                for acc, grad, out in ((accg, gg, dwg_ref), (accu, ug, dwu_ref)):
                    term = jnp.dot(normed_t[...], grad[:, columns], preferred_element_type=jnp.float32)
                    if weigh == "first":
                        acc[:, columns] = term
                    elif weigh == "more":
                        acc[:, columns] += term
                    else:
                        out[:, columns] = (acc[:, columns] + term).astype(out.dtype)
            return carry
        lax.fori_loop(0, n_tiles, body, 0, unroll=True)

    def part_copy(k):
        to = lax.rem(t + k, 4)
        start = pl.multiple_of(to * slice_rows, slice_rows)
        return pltpu.make_async_remote_copy(
            src_ref=part.at[pl.ds(start, slice_rows)], dst_ref=parts.at[k - 1],
            send_sem=psend.at[k - 1], recv_sem=precv.at[k - 1],
            device_id=(me, to), device_id_type=MESH,
        )

    def back():
        there = pl.ds(pl.multiple_of(y * rows, rows), rows)
        def body(n, carry):
            at = pl.ds(pl.multiple_of(n * TILE, TILE), TILE)
            dims = (((1,), (1,)), ((), ()))
            total = lax.dot_general(
                gg[there, :], wg[at, :], dims, preferred_element_type=jnp.float32
            ) + lax.dot_general(
                ug[there, :], wu[at, :], dims, preferred_element_type=jnp.float32
            )
            part[:, at] = total.astype(jnp.bfloat16)
            return carry
        lax.fori_loop(0, features // TILE, body, 0)
        for k in (1, 2, 3):
            part_copy(k).start()

    def finish_residual():
        for k in (1, 2, 3):
            part_copy(k).wait_recv()
        own = part[pl.ds(pl.multiple_of(t * slice_rows, slice_rows), slice_rows), :]
        total = own.astype(jnp.float32)
        for k in (0, 1, 2):
            total += parts[k].astype(jnp.float32)
        start = pl.multiple_of(me * rows + t * slice_rows, slice_rows)
        values = res[pl.ds(start, slice_rows), :].astype(jnp.float32)
        inverse = lax.rsqrt(jnp.mean(values * values, axis=-1, keepdims=True) + EPSILON)
        scaled = values * inverse
        weighted = total * gain_ref[...]
        mean = jnp.mean(weighted * scaled, axis=-1, keepdims=True)
        dres_ref[...] = ((weighted - scaled * mean) * inverse).astype(dres_ref.dtype)

    weights = [
        pltpu.make_async_copy(wg_hbm, wg, wsem.at[0]),
        pltpu.make_async_copy(wu_hbm, wu, wsem.at[1]),
    ]
    local = [
        pltpu.make_async_copy(
            res_ref, place(me, 0), lsem.at[0]
        ),
        pltpu.make_async_copy(
            hid_ref, hid.at[pl.ds(pl.multiple_of(me * rows, rows), rows)], lsem.at[1]
        ),
        pltpu.make_async_copy(gain_hbm, gain_ref, lsem.at[2]),
    ]
    for copy in local + weights:
        copy.start()

    barrier = pltpu.get_barrier_semaphore()
    for kind, there in directions(0):
        @pl.when(there)
        def _():
            pl.semaphore_signal(barrier, inc=1, device_id=(dest[kind], t), device_id_type=MESH)
    pl.semaphore_signal(barrier, inc=1, device_id=(other, t), device_id_type=MESH)
    for k in (1, 2, 3):
        pl.semaphore_signal(
            barrier, inc=1, device_id=(me, lax.rem(t + k, 4)), device_id_type=MESH
        )
    pl.semaphore_wait(
        barrier, 4 + jnp.where(z > 0, 1, 0) + jnp.where(z < last_z, 1, 0)
    )

    own_row, other_row = y * rows, (1 - y) * rows
    mates_start(me, own=True)
    send(0, 0)
    send(0, 1)
    for copy in local:
        copy.wait()
    forward(1, 0)
    from_across(0, 0)
    send(0, 2)
    mates_wait(me)
    norm_rows(z, own_row, rows)
    for copy in weights:
        copy.wait()
    factors(z, own_row, rows, 0, 2)
    forward(2, 0)
    factors(z, own_row, rows, 2, 4)
    forward(3, 0)
    forward(1, 1)
    forward_if(inner, 2, 1)
    from_across(1, 0)
    factors(z, own_row, rows, 4, n_tiles)
    forward(1, 2)
    forward_if(inner, 2, 2)
    from_across(2, 0)
    weigh_tiles(z, own_row, rows, None)
    back()
    from_across(3, 0)
    mates_wait(other)
    norm_rows(z, other_row, rows)
    factors(z, other_row, rows, 0, 4)
    forward_if(outer, 2, 1)
    forward_if(inner, 3, 1)
    factors(z, other_row, rows, 4, n_tiles)
    forward_if(outer, 2, 2)
    from_across(0, 1)
    from_across(0, 2)
    forward_if(inner, 3, 2)
    transpose_own()
    weigh_tiles(z, other_row, rows, "first")

    for j in (1, 2, 3):
        zz = order[j]
        mates_wait(zz * 2)
        mates_wait(zz * 2 + 1)
        norm_rows(zz, 0, 2 * rows)
        transpose_own()
        factors(zz, 0, 2 * rows, 0, 4)
        if j == 1:
            forward_if(outer, 3, 1)
        factors(zz, 0, 2 * rows, 4, n_tiles)
        if j == 1:
            forward_if(outer, 3, 2)
        if j == 3:
            finish_residual()
        from_across(j, 1)
        from_across(j, 2)
        weigh_tiles(zz, 0, 2 * rows, "last" if j == 3 else "more")

    for j in range(4):
        g = order[j] * 2 + y
        for p in (0, 1, 2):
            for kind, needed in directions(j):
                @pl.when(needed)
                def _():
                    route(g, p, kind, j == 0).wait_send()
            if not by_line(j, p):
                route(g, p, ACROSS, j == 0).wait_send()
        for k in (1, 2, 3):
            mate(g, k, j == 0).wait_send()
            mate(order[j] * 2 + 1 - y, k).wait_send()
    for kind, needed in line:
        @pl.when(needed)
        def _():
            route(other, 2, kind).wait_send()
    for k in (1, 2, 3):
        part_copy(k).wait_send()


def fused_shards(residual, norm_gain, gate_weight, up_weight, hidden_grad):
    slice_rows, features = residual.shape
    rows, wide = hidden_grad.shape
    n_dp = lax.axis_size("dp")
    depth = features // n_dp
    vmem = pl.BlockSpec(memory_space=pltpu.VMEM)
    hbm = pl.BlockSpec(memory_space=pltpu.HBM)
    low, high = jnp.bfloat16, jnp.float32
    dma = pltpu.SemaphoreType.DMA
    dres, dwg, dwu = pl.pallas_call(
        fused_kernel,
        out_shape=(
            jax.ShapeDtypeStruct((slice_rows, features), low),
            jax.ShapeDtypeStruct((depth, wide), low),
            jax.ShapeDtypeStruct((depth, wide), low),
        ),
        in_specs=[hbm] * 5,
        out_specs=(vmem, vmem, vmem),
        scratch_shapes=[
            pltpu.VMEM((1, features), high),
            pltpu.VMEM((2 * rows, wide), high),
            pltpu.VMEM((2 * rows, wide), high),
            pltpu.VMEM((features, wide), low),
            pltpu.VMEM((features, wide), low),
            pltpu.VMEM((n_dp * rows, features), low),
            pltpu.VMEM((n_dp * rows, wide), low),
            pltpu.VMEM((2 * rows, features), low),
            pltpu.VMEM((depth, 2 * rows), low),
            pltpu.VMEM((2 * rows, wide), low),
            pltpu.VMEM((2 * rows, wide), low),
            pltpu.VMEM((depth, wide), high),
            pltpu.VMEM((depth, wide), high),
            pltpu.VMEM((rows, features), low),
            pltpu.VMEM((3, slice_rows, features), low),
            dma((2,)),
            dma((3,)),
            dma((n_dp, 3, 3)),
            dma((n_dp, 3)),
            dma((n_dp, 3)),
            dma((n_dp, 3)),
            dma((3,)),
            dma((3,)),
        ],
        compiler_params=pltpu.CompilerParams(
            collective_id=0, has_side_effects=True, vmem_limit_bytes=56 * 1024 * 1024
        ),
    )(residual, hidden_grad, norm_gain.reshape(1, features), gate_weight, up_weight)
    factor = float(n_dp * rows) ** (-0.5)
    scale = lambda total: (total.astype(high) * factor).astype(low)
    return dres, scale(dwg), scale(dwu)


def solution(mesh):
    fits = mesh.shape["dp"] == 8 and mesh.shape["tensor"] == 4
    return jax.shard_map(
        fused_shards if fits else shards,
        mesh=mesh,
        in_specs=(
            P(("dp", "tensor"), None),
            P(),
            P(None, "tensor"),
            P(None, "tensor"),
            P("dp", "tensor"),
        ),
        out_specs=(P(("dp", "tensor"), None), P("dp", "tensor"), P("dp", "tensor")),
        check_vma=False,
    )
```
